32 devices in a mesh: freq: 2 (over x), row: 4 (over y, core), blk: 4 (over z).
Axes of the slice: x: 2, y: 2, z: 4, core: 2. Of those that a mesh axis runs over, the one named last changes fastest.
Arguments:
- counts: int32 [8192, 8, 128], P(('freq', 'row', 'blk')), parts along dimension 0, may hold values from 0 to 28, as said below
- subspace: bfloat16 [8192, 32], P(('freq', 'row', 'blk')), parts along dimension 0, may hold values from -6 to 6
Outputs:
- modes: float32 [8192, 32], P(('freq', 'row', 'blk')), parts along dimension 0
The draws below stay inside these ranges and needn't reach their ends.
There are 2 independent parts, one for each index of `freq`. The reference program is written for one: setup_inputs(seed, part) draws one part's arguments, and reference() takes and returns one part's arrays. A program takes and returns all parts, laid end to end along the dimension named above; each array names one. Nothing has to cross between parts.
Inputs may be any that keep to these rules, and one draw needn't show every extreme that they name: Integer spike counts.
All inputs are finite; a program needn't handle non-finite values.
Results may differ from the reference program's by a relative error of at most 0.008.
Values may be sent and summed in bfloat16 or wider, within the bound.
A program may use at most 64 MiB of HBM per device.

```python
import math
import jax
import jax.numpy as jnp
from jax import lax

SEGS = 8
TAPERS = 8
EPOCH_STEPS = 128
SPECTRAL_SLOT = 9
MODES = 32
NEURONS = 4096


def draw_counts(key, part):
    key_top, key_own, key_rhythm, key_weight = jax.random.split(key, 4)
    ceiling = jax.random.randint(key_top, (NEURONS, 1, 1), 2, 21)
    own_noise = jax.random.randint(key_own, (NEURONS, SEGS, EPOCH_STEPS), 0, ceiling)
    rhythm = jax.random.randint(key_rhythm, (MODES, SEGS, EPOCH_STEPS), 0, 4)
    device_clusters = jnp.arange(NEURONS, dtype=jnp.int32) // (NEURONS // MODES)
    weights = jax.random.randint(key_weight, (NEURONS, 1, 1), 0, 4)
    return (own_noise + weights * rhythm[device_clusters]).astype(jnp.int32)


def block_levels(rng, extent, pieces, smallest, high):
    def one(axis_at, parts):
        draws = jax.random.uniform(jax.random.fold_in(jax.random.fold_in(rng, 6), axis_at), (parts,), jnp.float32, smallest / len(pieces), high / len(pieces))
        return jnp.repeat(jnp.exp(draws), extent[axis_at] // parts).reshape((-1,) + (1,) * (len(extent) - axis_at - 1))

    level = one(*pieces[0])
    for cut in pieces[1:]:
        level = level * one(*cut)
    return level


def centred(key, extent, scale, reach, shards=(), held_as=jnp.bfloat16):
    drawn = jax.random.normal(key, extent, jnp.float32) * scale
    if len(shards) > 0:
        drawn = block_levels(key, extent, shards, -0.22, 0.18) * drawn
    return jnp.clip(drawn, min=-reach, max=reach).astype(held_as)


def setup_inputs(seed: int = 0, part: int = 0) -> dict:
    key_of = jax.random.split(jax.random.key(seed), 3)
    part_splits = jax.random.split(jax.random.fold_in(key_of[2], part), 3)
    return {
        "counts": draw_counts(jax.random.fold_in(jax.random.fold_in(key_of[2], part), 71), part),
        "subspace": centred(part_splits[1], (NEURONS, MODES), 1.0, 6.0, ((0, 16),)),
    }


def spectral_table():
    clock_moments = jnp.arange(EPOCH_STEPS, dtype=jnp.float32)
    window_degrees = jnp.arange(TAPERS, dtype=jnp.float32) + 1.0
    prolate_windows = jnp.sqrt(2.0 / (EPOCH_STEPS + 1.0)) * jnp.sin(jnp.pi * (clock_moments[:, None] + 1.0) * window_degrees[None, :] / (EPOCH_STEPS + 1.0))
    oscillation_radians = 2.0 * jnp.pi * SPECTRAL_SLOT * clock_moments / EPOCH_STEPS
    return jnp.concatenate([prolate_windows * jnp.cos(oscillation_radians)[:, None], -prolate_windows * jnp.sin(oscillation_radians)[:, None]], axis=1)

def make_spectra(counts):
    values = counts.astype(jnp.float32)
    centered = values - lax.optimization_barrier(jnp.mean(values, axis=2, keepdims=True))
    height = counts.shape[0]
    flattened = centered.reshape(height * SEGS, EPOCH_STEPS)
    result = jnp.dot(flattened.astype(jnp.float32), spectral_table().astype(jnp.float32), precision=lax.Precision.HIGHEST, preferred_element_type=jnp.float32)
    return result.reshape(height, SEGS * 2 * TAPERS).astype(jnp.bfloat16)

def twist(spectra):
    height = spectra.shape[0]
    pieces_view = spectra.reshape(height, SEGS, 2, TAPERS)
    return jnp.stack([pieces_view[:, :, 1], -pieces_view[:, :, 0]], axis=2).reshape(height, SEGS * 2 * TAPERS)

def inverse_power(spectra):
    widened = spectra.astype(jnp.float32)
    return 1.0 / (lax.optimization_barrier(jnp.sum(widened * widened, axis=1)) + 1e-05)

def tile_image(stacked, inverse_rows, column_spectra, inverse_cols, column_subspace):
    height = inverse_rows.shape[0]
    products = lax.dot_general(stacked.astype(jnp.float32), column_spectra.astype(jnp.float32), (((1,), (1,)), ((), ())), preferred_element_type=jnp.float32)
    real_part = products[:height]
    imag_part = products[height:]
    squared = (real_part * real_part + imag_part * imag_part) * inverse_rows[:, None] * inverse_cols[None, :]
    degrees = float(SEGS * TAPERS)
    coherence = jnp.maximum((degrees * squared - 1.0) / (degrees - 1.0), 0.0).astype(jnp.bfloat16)
    return jnp.dot(coherence.astype(jnp.float32), column_subspace.astype(jnp.float32), preferred_element_type=jnp.float32)

def reference(counts, subspace):
    spectra = make_spectra(counts)
    inverse_factor = inverse_power(spectra)
    twisted = twist(spectra)
    neuron_total = spectra.shape[0]
    rows_per_block = math.gcd(neuron_total, 1024)
    turns = neuron_total // rows_per_block

    def one_block(position):
        offset = (position * rows_per_block).astype(jnp.int32)
        rows_here = lax.dynamic_slice_in_dim(spectra, offset, rows_per_block, 0)
        twist_here = lax.dynamic_slice_in_dim(twisted, offset, rows_per_block, 0)
        inverse_here = lax.dynamic_slice_in_dim(inverse_factor, offset, rows_per_block, 0)
        stacked = jnp.concatenate([rows_here, twist_here], axis=0)
        return tile_image(stacked, inverse_here, spectra, inverse_factor, subspace)
    projected = lax.map(one_block, jnp.arange(turns, dtype=jnp.int32)).reshape(neuron_total, MODES)
    gram = jnp.dot(projected.T.astype(jnp.float32), projected.astype(jnp.float32), precision=lax.Precision.HIGHEST, preferred_element_type=jnp.float32)
    factor = jnp.linalg.cholesky(gram)
    solved = jax.scipy.linalg.solve_triangular(factor, projected.T, lower=True)
    return solved.T * jnp.sqrt(jnp.float32(neuron_total))
```

```python
import functools
import math

import jax
import jax.numpy as jnp
import ml_dtypes
import numpy as np
from jax import lax
from jax.experimental import pallas as pl
from jax.experimental.pallas import tpu as pltpu
from jax.sharding import PartitionSpec as P

SEGS = 8
TAPERS = 8
EPOCH_STEPS = 128
SPECTRAL_SLOT = 9
MODES = 32
WIDTH = SEGS * 2 * TAPERS
MESH = pl.DeviceIdType.MESH


def centred_table():
    t = np.arange(EPOCH_STEPS, dtype=np.float64)
    k = np.arange(TAPERS, dtype=np.float64) + 1.0
    h = np.sqrt(2.0 / (EPOCH_STEPS + 1.0)) * np.sin(
        np.pi * (t[:, None] + 1.0) * k[None, :] / (EPOCH_STEPS + 1.0)
    )
    angle = 2.0 * np.pi * SPECTRAL_SLOT * t / EPOCH_STEPS
    table = np.concatenate([h * np.cos(angle)[:, None], -h * np.sin(angle)[:, None]], axis=1)
    return table - table.mean(axis=0, keepdims=True)


def split_table():
    table = centred_table()
    whole = np.zeros((SEGS * EPOCH_STEPS, WIDTH))
    for s in range(SEGS):
        whole[s * EPOCH_STEPS : (s + 1) * EPOCH_STEPS, s * 2 * TAPERS : (s + 1) * 2 * TAPERS] = table
    pieces = []
    rest = whole
    for _ in range(3):
        piece = rest.astype(ml_dtypes.bfloat16)
        pieces.append(piece)
        rest = rest - piece.astype(np.float64)
    return np.concatenate(pieces, axis=1)


def twist_matrix():
    m = np.zeros((WIDTH, WIDTH), np.float32)
    for s in range(SEGS):
        for c in range(TAPERS):
            re, im = s * 2 * TAPERS + c, s * 2 * TAPERS + TAPERS + c
            m[im, re] = 1.0
            m[re, im] = -1.0
    return m.astype(ml_dtypes.bfloat16)


def each(first, last, body):
    if last - first <= 16:
        for i in range(first, last):
            body(i)
    else:
        lax.fori_loop(first, last, lambda i, c: (body(i), c)[1], 0)


def nt(a, b, precision=None):
    return lax.dot_general(
        a, b, (((1,), (1,)), ((), ())), precision=precision, preferred_element_type=jnp.float32
    )


def kernel(
    nr, nb, counts, sub_t, table, twist, out,
    xs, tab, rows, twisted, irow, cols, subs, part, landed, grams,
    x_sem, t_sem, row_send, row_recv, col_send, col_recv, sub_send, sub_recv,
    part_send, part_recv, gram_send, gram_recv,
):
    my_row, my_blk = lax.axis_index("row"), lax.axis_index("blk")
    height = rows.shape[1]

    def peer(dr, db):
        return {"row": lax.rem(my_row + dr, nr), "blk": lax.rem(my_blk + db, nb)}

    loads = [pltpu.make_async_copy(counts.at[:, s], xs.at[s], x_sem.at[s]) for s in range(SEGS)]
    table_load = pltpu.make_async_copy(table, tab, t_sem)
    table_load.start()
    for load in loads:
        load.start()

    barrier = pltpu.get_barrier_semaphore()
    each(1, nr * nb, lambda k: pl.semaphore_signal(
        barrier, inc=1, device_id=peer(k // nb, k % nb), device_id_type=MESH))

    subs[0] = sub_t[...]
    table_load.wait()
    total = jnp.zeros((height, 3 * WIDTH), jnp.float32)
    for s in range(0, SEGS, 2):
        loads[s].wait()
        loads[s + 1].wait()
        x = jnp.concatenate([xs[s], xs[s + 1]], axis=1).astype(jnp.float32).astype(jnp.bfloat16)
        total += jnp.dot(
            x, tab[s * EPOCH_STEPS : (s + 2) * EPOCH_STEPS], preferred_element_type=jnp.float32
        )
    spectra = (total[:, 2 * WIDTH :] + total[:, WIDTH : 2 * WIDTH]) + total[:, :WIDTH]
    spectra = spectra.astype(jnp.bfloat16)
    rows[0] = spectra
    cols[0] = spectra

    pl.semaphore_wait(barrier, nr * nb - 1)

    def col_copy(d):
        return pltpu.make_async_remote_copy(
            src_ref=rows.at[0], dst_ref=cols.at[d], send_sem=col_send.at[d],
            recv_sem=col_recv.at[d], device_id=peer(0, d), device_id_type=MESH)

    def sub_copy(d):
        return pltpu.make_async_remote_copy(
            src_ref=subs.at[0], dst_ref=subs.at[d], send_sem=sub_send.at[d],
            recv_sem=sub_recv.at[d], device_id=peer(0, d), device_id_type=MESH)

    def row_copy(d):
        return pltpu.make_async_remote_copy(
            src_ref=rows.at[0], dst_ref=rows.at[d], send_sem=row_send.at[d],
            recv_sem=row_recv.at[d], device_id=peer(d, 0), device_id_type=MESH)

    def part_copy(d):
        return pltpu.make_async_remote_copy(
            src_ref=part.at[d], dst_ref=landed.at[d], send_sem=part_send.at[d],
            recv_sem=part_recv.at[d], device_id=peer(nr - d, 0), device_id_type=MESH)

    def gram_copy(k):
        return pltpu.make_async_remote_copy(
            src_ref=grams.at[0], dst_ref=grams.at[k], send_sem=gram_send.at[k],
            recv_sem=gram_recv.at[k], device_id=peer(k // nb, k % nb), device_id_type=MESH)

    each(1, nr, lambda d: row_copy(d).start())

    def send_cols(d):
        col_copy(d).start()
        sub_copy(d).start()

    each(1, nb, send_cols)

    degrees = float(SEGS * TAPERS)
    ones = jnp.ones((8, WIDTH), jnp.float32)

    def prepare_row(r):
        here = rows[r]
        twisted[r] = jnp.dot(here, twist[...], preferred_element_type=jnp.float32).astype(jnp.bfloat16)
        wide = here.astype(jnp.float32)
        power = nt(ones, wide * wide, lax.Precision.HIGHEST)
        irow[r] = (degrees / (degrees - 1.0)) / (power + 1e-05)

    def column(d):
        wide = cols[d].astype(jnp.float32)
        return 1.0 / (jnp.sum(wide * wide, axis=1, keepdims=True) + 1e-05)

    def tile(d, r, icol):
        here = cols[d]
        re = nt(here, rows[r])
        im = nt(here, twisted[r])
        msc = (re * re + im * im) * icol * irow[r, 0:1]
        coherence = jnp.maximum(msc - 1.0 / (degrees - 1.0), 0.0).astype(jnp.bfloat16)
        return jnp.dot(subs[d], coherence, preferred_element_type=jnp.float32)

    own = column(0)
    for r in range(nr):
        if r > 0:
            row_copy(r).wait()
        prepare_row(r)
        part[r] = tile(0, r, own)

    def add_column(d, final):
        col_copy(d).wait()
        sub_copy(d).wait()
        icol = column(d)
        for r in list(range(1, nr)) + [0]:
            part[r] += tile(d, r, icol)
            if final and r > 0:
                part_copy(r).start()

    each(1, nb - 1, lambda d: add_column(d, False))
    add_column(nb - 1, True)

    image = part[0]
    for r in range(1, nr):
        part_copy(r).wait()
        image += landed[r]

    gram = nt(image, image, lax.Precision.HIGHEST)
    quarter = MODES // 4
    grams[0] = jnp.concatenate([gram[q * quarter : (q + 1) * quarter] for q in range(4)], axis=1)
    each(1, nr * nb, lambda k: gram_copy(k).start())
    each(1, nr * nb, lambda k: gram_copy(k).wait())
    packed = jnp.sum(grams[...], axis=0)
    gram = jnp.concatenate([packed[:, q * MODES : (q + 1) * MODES] for q in range(4)], axis=0)

    sub_id = lax.broadcasted_iota(jnp.int32, (MODES, 2 * MODES), 0)
    lane_id = lax.broadcasted_iota(jnp.int32, (MODES, 2 * MODES), 1)
    eye = (sub_id == lane_id).astype(jnp.float32)
    work = jnp.concatenate([eye[:, :MODES], gram], axis=1)
    for k in range(MODES - 1):
        top = work[k : k + 1]
        pivot = work[k : k + 1, MODES + k : MODES + k + 1]
        below = work[:, MODES + k : MODES + k + 1]
        update = below * (top * (1.0 / pivot))
        work = work - jnp.where(sub_id > k, update, 0.0)
    pivots = jnp.sum(jnp.where(lane_id == sub_id + MODES, work, 0.0), axis=1, keepdims=True)
    neurons = float(height * nr * nb)
    inverse = work[:, :MODES] * (math.sqrt(neurons) / jnp.sqrt(pivots))
    out[...] = jnp.dot(
        inverse, image, precision=lax.Precision.HIGHEST, preferred_element_type=jnp.float32
    )


def local(nr, nb, counts, subspace):
    height = counts.shape[0]
    vmem = pl.BlockSpec(memory_space=pltpu.VMEM)
    hbm = pl.BlockSpec(memory_space=pl.ANY)
    dma = pltpu.SemaphoreType.DMA
    modes_t = pl.pallas_call(
        functools.partial(kernel, nr, nb),
        out_shape=jax.ShapeDtypeStruct((MODES, height), jnp.float32),
        in_specs=[hbm, vmem, hbm, vmem],
        out_specs=vmem,
        scratch_shapes=[
            pltpu.VMEM((SEGS, height, EPOCH_STEPS), jnp.int32),
            pltpu.VMEM((SEGS * EPOCH_STEPS, 3 * WIDTH), jnp.bfloat16),
            pltpu.VMEM((nr, height, WIDTH), jnp.bfloat16),
            pltpu.VMEM((nr, height, WIDTH), jnp.bfloat16),
            pltpu.VMEM((nr, 8, height), jnp.float32),
            pltpu.VMEM((nb, height, WIDTH), jnp.bfloat16),
            pltpu.VMEM((nb, MODES, height), jnp.bfloat16),
            pltpu.VMEM((nr, MODES, height), jnp.float32),
            pltpu.VMEM((nr, MODES, height), jnp.float32),
            pltpu.VMEM((nr * nb, MODES // 4, 4 * MODES), jnp.float32),
            dma((SEGS,)), dma,
            dma((nr,)), dma((nr,)),
            dma((nb,)), dma((nb,)), dma((nb,)), dma((nb,)),
            dma((nr,)), dma((nr,)),
            dma((nr * nb,)), dma((nr * nb,)),
        ],
        compiler_params=pltpu.CompilerParams(
            collective_id=0, has_side_effects=True, vmem_limit_bytes=40 * 1024 * 1024
        ),
        name="subspace_step",
    )(counts, subspace.T, jnp.asarray(split_table()), jnp.asarray(twist_matrix()))
    return modes_t.T


def solution(mesh):
    nr, nb = mesh.shape["row"], mesh.shape["blk"]
    return jax.shard_map(
        functools.partial(local, nr, nb),
        mesh=mesh,
        in_specs=(P(("freq", "row", "blk"), None, None), P(("freq", "row", "blk"), None)),
        out_specs=P(("freq", "row", "blk"), None),
        check_vma=False,
    )
```

```python
import functools
import math

import jax
import jax.numpy as jnp
import ml_dtypes
import numpy as np
from jax import lax
from jax.experimental import pallas as pl
from jax.experimental.pallas import tpu as pltpu
from jax.sharding import PartitionSpec as P

SEGS = 8
TAPERS = 8
EPOCH_STEPS = 128
SPECTRAL_SLOT = 9
MODES = 32
WIDTH = SEGS * 2 * TAPERS
MESH = pl.DeviceIdType.MESH


def centred_table():
    t = np.arange(EPOCH_STEPS, dtype=np.float64)
    k = np.arange(TAPERS, dtype=np.float64) + 1.0
    h = np.sqrt(2.0 / (EPOCH_STEPS + 1.0)) * np.sin(
        np.pi * (t[:, None] + 1.0) * k[None, :] / (EPOCH_STEPS + 1.0)
    )
    angle = 2.0 * np.pi * SPECTRAL_SLOT * t / EPOCH_STEPS
    table = np.concatenate([h * np.cos(angle)[:, None], -h * np.sin(angle)[:, None]], axis=1)
    return table - table.mean(axis=0, keepdims=True)


def split_table():
    table = centred_table()
    whole = np.zeros((SEGS * EPOCH_STEPS, WIDTH))
    for s in range(SEGS):
        whole[s * EPOCH_STEPS : (s + 1) * EPOCH_STEPS, s * 2 * TAPERS : (s + 1) * 2 * TAPERS] = table
    pieces = []
    rest = whole
    for _ in range(3):
        piece = rest.astype(ml_dtypes.bfloat16)
        pieces.append(piece)
        rest = rest - piece.astype(np.float64)
    return np.concatenate(pieces, axis=1)


def twist_matrix():
    source = lax.broadcasted_iota(jnp.int32, (WIDTH, WIDTH), 0)
    target = lax.broadcasted_iota(jnp.int32, (WIDTH, WIDTH), 1)
    real = lax.rem(target, 2 * TAPERS) < TAPERS
    plus = jnp.where(real & (source == target + TAPERS), 1.0, 0.0)
    minus = jnp.where(jnp.logical_not(real) & (source == target - TAPERS), 1.0, 0.0)
    return (plus - minus).astype(jnp.bfloat16)


def each(first, last, body):
    if last - first <= 16:
        for i in range(first, last):
            body(i)
    else:
        lax.fori_loop(first, last, lambda i, c: (body(i), c)[1], 0)


def nt(a, b, precision=None):
    return lax.dot_general(
        a, b, (((1,), (1,)), ((), ())), precision=precision, preferred_element_type=jnp.float32
    )


def kernel(
    nr, nb, counts, sub_t, table, out,
    xs, tab, rows, twisted, irow, cols, subs, part, landed, grams,
    x_sem, t_sem, s_sem, row_send, row_recv, col_send, col_recv, sub_send, sub_recv,
    part_send, part_recv, gram_send, gram_recv,
):
    my_row, my_blk = lax.axis_index("row"), lax.axis_index("blk")
    height = rows.shape[1]

    def peer(dr, db):
        return {"row": lax.rem(my_row + dr, nr), "blk": lax.rem(my_blk + db, nb)}

    upper = (2 * my_blk) // nb
    place = my_blk + upper * (nb - 1 - 2 * my_blk)

    def near(j):
        u = j + (j - place + nb) // nb
        return u + upper * (nb - 1 - 2 * u)

    def sent(j):
        return lax.rem(near(j) - my_blk + nb, nb)

    def taken(j):
        return lax.rem(my_blk - near(j) + nb, nb)

    barrier = pltpu.get_barrier_semaphore()
    each(1, nb, lambda d: pl.semaphore_signal(
        barrier, inc=1, device_id=peer(0, d), device_id_type=MESH))
    each(1, nr, lambda d: pl.semaphore_signal(
        barrier, inc=1, device_id=peer(d, 0), device_id_type=MESH))

    loads = [pltpu.make_async_copy(counts.at[:, s], xs.at[s], x_sem.at[s]) for s in range(SEGS)]
    table_load = pltpu.make_async_copy(table, tab, t_sem)
    table_load.start()
    sub_load = pltpu.make_async_copy(sub_t, subs.at[0], s_sem)
    sub_load.start()
    for load in loads:
        load.start()

    table_load.wait()
    total = jnp.zeros((height, 3 * WIDTH), jnp.float32)
    for s in range(0, SEGS, 2):
        loads[s].wait()
        loads[s + 1].wait()
        x = jnp.concatenate([xs[s], xs[s + 1]], axis=1).astype(jnp.float32).astype(jnp.bfloat16)
        total += jnp.dot(
            x, tab[s * EPOCH_STEPS : (s + 2) * EPOCH_STEPS], preferred_element_type=jnp.float32
        )
    spectra = (total[:, 2 * WIDTH :] + total[:, WIDTH : 2 * WIDTH]) + total[:, :WIDTH]
    spectra = spectra.astype(jnp.bfloat16)
    rows[0] = spectra
    cols[0] = spectra

    pl.semaphore_wait(barrier, nr + nb - 2)

    sub_load.wait()

    def col_copy(d):
        return pltpu.make_async_remote_copy(
            src_ref=rows.at[0], dst_ref=cols.at[d], send_sem=col_send.at[d],
            recv_sem=col_recv.at[d], device_id=peer(0, d), device_id_type=MESH)

    def sub_copy(d):
        return pltpu.make_async_remote_copy(
            src_ref=subs.at[0], dst_ref=subs.at[d], send_sem=sub_send.at[d],
            recv_sem=sub_recv.at[d], device_id=peer(0, d), device_id_type=MESH)

    def row_copy(d):
        return pltpu.make_async_remote_copy(
            src_ref=rows.at[0], dst_ref=rows.at[d], send_sem=row_send.at[d],
            recv_sem=row_recv.at[d], device_id=peer(d, 0), device_id_type=MESH)

    def part_copy(d):
        return pltpu.make_async_remote_copy(
            src_ref=part.at[d], dst_ref=landed.at[d], send_sem=part_send.at[d],
            recv_sem=part_recv.at[d], device_id=peer(nr - d, 0), device_id_type=MESH)

    def gram_copy(dr, db):
        k = dr * nb + db
        return pltpu.make_async_remote_copy(
            src_ref=grams.at[0], dst_ref=grams.at[k], send_sem=gram_send.at[k],
            recv_sem=gram_recv.at[k], device_id=peer(dr, db), device_id_type=MESH)

    def send_cols(j):
        d = sent(nb - 2 - j)
        sub_copy(d).start()
        col_copy(d).start()

    each(0, nb - 1, send_cols)
    each(1, nr, lambda d: row_copy(d).start())

    degrees = float(SEGS * TAPERS)
    ones = jnp.ones((8, WIDTH), jnp.float32)
    twist = twist_matrix()

    def prepare_row(r):
        here = rows[r]
        twisted[r] = jnp.dot(here, twist, preferred_element_type=jnp.float32).astype(jnp.bfloat16)
        wide = here.astype(jnp.float32)
        power = nt(ones, wide * wide, lax.Precision.HIGHEST)
        irow[r] = (degrees / (degrees - 1.0)) / (power + 1e-05)

    def column(d):
        wide = cols[d].astype(jnp.float32)
        return 1.0 / (jnp.sum(wide * wide, axis=1, keepdims=True) + 1e-05)

    def tile(d, r, icol):
        here = cols[d]
        re = nt(here, rows[r])
        im = nt(here, twisted[r])
        msc = (re * re + im * im) * icol * irow[r, 0:1]
        coherence = jnp.maximum(msc - 1.0 / (degrees - 1.0), 0.0).astype(jnp.bfloat16)
        return jnp.dot(subs[d], coherence, preferred_element_type=jnp.float32)

    own = column(0)
    for r in range(nr):
        if r > 0:
            row_copy(r).wait_recv()
        prepare_row(r)
        part[r] = tile(0, r, own)

    def add_column(j, final):
        d = taken(j)
        sub_copy(d).wait_recv()
        col_copy(d).wait_recv()
        icol = column(d)
        for r in list(range(1, nr)) + [0]:
            part[r] += tile(d, r, icol)
            if final and r > 0:
                part_copy(r).start()

    each(0, nb - 2, lambda j: add_column(j, False))
    add_column(nb - 2, True)

    image = part[0]
    for r in range(1, nr):
        part_copy(r).wait_recv()
        image += landed[r]

    gram = nt(image, image, lax.Precision.HIGHEST)
    quarter = MODES // 4
    grams[0] = jnp.concatenate([gram[q * quarter : (q + 1) * quarter] for q in range(4)], axis=1)

    def send_gram(j):
        d = sent(nb - 2 - j)
        for dr in range(nr):
            gram_copy(dr, d).start()

    each(0, nb - 1, send_gram)
    each(1, nr, lambda d: gram_copy(d, 0).start())
    each(1, nr * nb, lambda k: gram_copy(k // nb, k % nb).wait_recv())
    packed = jnp.sum(grams[...], axis=0)
    gram = jnp.concatenate([packed[:, q * MODES : (q + 1) * MODES] for q in range(4)], axis=0)

    sub_id = lax.broadcasted_iota(jnp.int32, (MODES, 2 * MODES), 0)
    lane_id = lax.broadcasted_iota(jnp.int32, (MODES, 2 * MODES), 1)
    eye = (sub_id == lane_id).astype(jnp.float32)
    work = jnp.concatenate([eye[:, :MODES], gram], axis=1)
    for k in range(0, MODES, 2):
        c = MODES + k
        first, second = work[k : k + 1], work[k + 1 : k + 2]
        left, right = work[:, c : c + 1], work[:, c + 1 : c + 2]
        scaled = first * (1.0 / work[k : k + 1, c : c + 1])
        cross = scaled[:, c + 1 : c + 2]
        second = second - scaled * work[k + 1 : k + 2, c : c + 1]
        right = right - left * cross
        second = second * (1.0 / second[:, c + 1 : c + 2])
        work = work - jnp.where(sub_id > k, left, 0.0) * scaled - jnp.where(sub_id > k + 1, right, 0.0) * second
    pivots = jnp.sum(jnp.where(lane_id == sub_id + MODES, work, 0.0), axis=1, keepdims=True)
    neurons = float(height * nr * nb)
    inverse = work[:, :MODES] * (math.sqrt(neurons) / jnp.sqrt(pivots))
    out[...] = jnp.dot(
        inverse, image, precision=lax.Precision.HIGHEST, preferred_element_type=jnp.float32
    )

    def sent_cols(d):
        sub_copy(d).wait_send()
        col_copy(d).wait_send()

    def sent_rows(d):
        row_copy(d).wait_send()
        part_copy(d).wait_send()

    each(1, nb, sent_cols)
    each(1, nr, sent_rows)
    each(1, nr * nb, lambda k: gram_copy(k // nb, k % nb).wait_send())


def local(nr, nb, counts, subspace):
    height = counts.shape[0]
    vmem = pl.BlockSpec(memory_space=pltpu.VMEM)
    hbm = pl.BlockSpec(memory_space=pl.ANY)
    dma = pltpu.SemaphoreType.DMA
    modes_t = pl.pallas_call(
        functools.partial(kernel, nr, nb),
        out_shape=jax.ShapeDtypeStruct((MODES, height), jnp.float32),
        in_specs=[hbm, hbm, hbm],
        out_specs=vmem,
        scratch_shapes=[
            pltpu.VMEM((SEGS, height, EPOCH_STEPS), jnp.int32),
            pltpu.VMEM((SEGS * EPOCH_STEPS, 3 * WIDTH), jnp.bfloat16),
            pltpu.VMEM((nr, height, WIDTH), jnp.bfloat16),
            pltpu.VMEM((nr, height, WIDTH), jnp.bfloat16),
            pltpu.VMEM((nr, 8, height), jnp.float32),
            pltpu.VMEM((nb, height, WIDTH), jnp.bfloat16),
            pltpu.VMEM((nb, MODES, height), jnp.bfloat16),
            pltpu.VMEM((nr, MODES, height), jnp.float32),
            pltpu.VMEM((nr, MODES, height), jnp.float32),
            pltpu.VMEM((nr * nb, MODES // 4, 4 * MODES), jnp.float32),
            dma((SEGS,)), dma, dma,
            dma((nr,)), dma((nr,)),
            dma((nb,)), dma((nb,)), dma((nb,)), dma((nb,)),
            dma((nr,)), dma((nr,)),
            dma((nr * nb,)), dma((nr * nb,)),
        ],
        compiler_params=pltpu.CompilerParams(
            collective_id=0, has_side_effects=True, vmem_limit_bytes=40 * 1024 * 1024
        ),
        name="subspace_step",
    )(counts, subspace.T, jnp.asarray(split_table()))
    return modes_t.T


def solution(mesh):
    nr, nb = mesh.shape["row"], mesh.shape["blk"]
    return jax.shard_map(
        functools.partial(local, nr, nb),
        mesh=mesh,
        in_specs=(P(("freq", "row", "blk"), None, None), P(("freq", "row", "blk"), None)),
        out_specs=P(("freq", "row", "blk"), None),
        check_vma=False,
    )
```

```python
import functools
import math

import jax
import jax.numpy as jnp
import ml_dtypes
import numpy as np
from jax import lax
from jax.experimental import pallas as pl
from jax.experimental.pallas import tpu as pltpu
from jax.sharding import PartitionSpec as P

SEGS = 8
TAPERS = 8
EPOCH_STEPS = 128
SPECTRAL_SLOT = 9
MODES = 32
WIDTH = SEGS * 2 * TAPERS
MESH = pl.DeviceIdType.MESH


def centred_table():
    t = np.arange(EPOCH_STEPS, dtype=np.float64)
    k = np.arange(TAPERS, dtype=np.float64) + 1.0
    h = np.sqrt(2.0 / (EPOCH_STEPS + 1.0)) * np.sin(
        np.pi * (t[:, None] + 1.0) * k[None, :] / (EPOCH_STEPS + 1.0)
    )
    angle = 2.0 * np.pi * SPECTRAL_SLOT * t / EPOCH_STEPS
    table = np.concatenate([h * np.cos(angle)[:, None], -h * np.sin(angle)[:, None]], axis=1)
    return table - table.mean(axis=0, keepdims=True)


def split_table():
    table = centred_table()
    whole = np.zeros((SEGS * EPOCH_STEPS, WIDTH))
    for s in range(SEGS):
        whole[s * EPOCH_STEPS : (s + 1) * EPOCH_STEPS, s * 2 * TAPERS : (s + 1) * 2 * TAPERS] = table
    pieces = []
    rest = whole
    for _ in range(3):
        piece = rest.astype(ml_dtypes.bfloat16)
        pieces.append(piece)
        rest = rest - piece.astype(np.float64)
    return np.concatenate(pieces, axis=1)


def twist_matrix():
    source = lax.broadcasted_iota(jnp.int32, (WIDTH, WIDTH), 0)
    target = lax.broadcasted_iota(jnp.int32, (WIDTH, WIDTH), 1)
    real = lax.rem(target, 2 * TAPERS) < TAPERS
    plus = jnp.where(real & (source == target + TAPERS), 1.0, 0.0)
    minus = jnp.where(jnp.logical_not(real) & (source == target - TAPERS), 1.0, 0.0)
    return (plus - minus).astype(jnp.bfloat16)


def each(first, last, body):
    if last - first <= 16:
        for i in range(first, last):
            body(i)
    else:
        lax.fori_loop(first, last, lambda i, c: (body(i), c)[1], 0)


def nt(a, b, precision=None):
    return lax.dot_general(
        a, b, (((1,), (1,)), ((), ())), precision=precision, preferred_element_type=jnp.float32
    )


def kernel(
    nr, nb, counts, sub_t, table, out,
    xs, tab, rows, twisted, irow, cols, subs, part, landed, grams,
    x_sem, t_sem, s_sem, row_send, row_recv, col_send, col_recv, sub_send, sub_recv,
    part_send, part_recv, gram_send, gram_recv,
):
    my_row, my_blk = lax.axis_index("row"), lax.axis_index("blk")
    height = rows.shape[1]

    def peer(dr, db):
        return {"row": lax.rem(my_row + dr, nr), "blk": lax.rem(my_blk + db, nb)}

    upper = (2 * my_blk) // nb
    place = my_blk + upper * (nb - 1 - 2 * my_blk)

    def near(j):
        u = j + (j - place + nb) // nb
        return u + upper * (nb - 1 - 2 * u)

    def sent(j):
        return lax.rem(near(j) - my_blk + nb, nb)

    def taken(j):
        return lax.rem(my_blk - near(j) + nb, nb)

    barrier = pltpu.get_barrier_semaphore()
    each(1, nb, lambda d: pl.semaphore_signal(
        barrier, inc=1, device_id=peer(0, d), device_id_type=MESH))
    each(1, nr, lambda d: pl.semaphore_signal(
        barrier, inc=1, device_id=peer(d, 0), device_id_type=MESH))

    loads = [pltpu.make_async_copy(counts.at[:, s], xs.at[s], x_sem.at[s]) for s in range(SEGS)]
    table_load = pltpu.make_async_copy(table, tab, t_sem)
    table_load.start()
    sub_load = pltpu.make_async_copy(sub_t, subs.at[0], s_sem)
    sub_load.start()
    for load in loads:
        load.start()

    table_load.wait()
    total = jnp.zeros((height, 3 * WIDTH), jnp.float32)
    for s in range(0, SEGS, 2):
        loads[s].wait()
        loads[s + 1].wait()
        x = jnp.concatenate([xs[s], xs[s + 1]], axis=1).astype(jnp.float32).astype(jnp.bfloat16)
        total += jnp.dot(
            x, tab[s * EPOCH_STEPS : (s + 2) * EPOCH_STEPS], preferred_element_type=jnp.float32
        )
    spectra = (total[:, 2 * WIDTH :] + total[:, WIDTH : 2 * WIDTH]) + total[:, :WIDTH]
    spectra = spectra.astype(jnp.bfloat16)
    rows[0] = spectra
    cols[0] = spectra

    pl.semaphore_wait(barrier, nr + nb - 2)

    sub_load.wait()

    def col_copy(d):
        return pltpu.make_async_remote_copy(
            src_ref=rows.at[0], dst_ref=cols.at[d], send_sem=col_send.at[d],
            recv_sem=col_recv.at[d], device_id=peer(0, d), device_id_type=MESH)

    def sub_copy(d):
        return pltpu.make_async_remote_copy(
            src_ref=subs.at[0], dst_ref=subs.at[d], send_sem=sub_send.at[d],
            recv_sem=sub_recv.at[d], device_id=peer(0, d), device_id_type=MESH)

    def row_copy(d):
        return pltpu.make_async_remote_copy(
            src_ref=rows.at[0], dst_ref=rows.at[d], send_sem=row_send.at[d],
            recv_sem=row_recv.at[d], device_id=peer(d, 0), device_id_type=MESH)

    def part_copy(d):
        return pltpu.make_async_remote_copy(
            src_ref=part.at[d], dst_ref=landed.at[d], send_sem=part_send.at[d],
            recv_sem=part_recv.at[d], device_id=peer(nr - d, 0), device_id_type=MESH)

    def gram_copy(dr, db):
        k = dr * nb + db
        return pltpu.make_async_remote_copy(
            src_ref=grams.at[0], dst_ref=grams.at[k], send_sem=gram_send.at[k],
            recv_sem=gram_recv.at[k], device_id=peer(dr, db), device_id_type=MESH)

    def send_cols(j):
        d = sent(nb - 2 - j)
        sub_copy(d).start()
        col_copy(d).start()

    each(0, nb - 1, send_cols)
    each(1, nr, lambda d: row_copy(d).start())

    degrees = float(SEGS * TAPERS)
    ones = jnp.ones((8, WIDTH), jnp.float32)
    twist = twist_matrix()

    def prepare_row(r):
        here = rows[r]
        twisted[r] = jnp.dot(here, twist, preferred_element_type=jnp.float32).astype(jnp.bfloat16)
        wide = here.astype(jnp.float32)
        power = nt(ones, wide * wide, lax.Precision.HIGHEST)
        irow[r] = (degrees / (degrees - 1.0)) / (power + 1e-05)

    def column(d):
        wide = cols[d].astype(jnp.float32)
        return 1.0 / (jnp.sum(wide * wide, axis=1, keepdims=True) + 1e-05)

    def tile(d, r, icol):
        here = cols[d]
        re = nt(here, rows[r])
        im = nt(here, twisted[r])
        msc = (re * re + im * im) * icol * irow[r, 0:1]
        coherence = jnp.maximum(msc - 1.0 / (degrees - 1.0), 0.0).astype(jnp.bfloat16)
        return jnp.dot(subs[d], coherence, preferred_element_type=jnp.float32)

    own = column(0)
    for r in range(nr):
        if r > 0:
            row_copy(r).wait_recv()
        prepare_row(r)
        part[r] = tile(0, r, own)

    def add_column(j, final):
        d = taken(j)
        sub_copy(d).wait_recv()
        col_copy(d).wait_recv()
        icol = column(d)
        for r in list(range(1, nr)) + [0]:
            part[r] += tile(d, r, icol)
            if final and r > 0:
                part_copy(r).start()

    each(0, nb - 2, lambda j: add_column(j, False))
    add_column(nb - 2, True)

    image = part[0]
    for r in range(1, nr):
        part_copy(r).wait_recv()
        image += landed[r]

    gram = nt(image, image, lax.Precision.HIGHEST)
    quarter = MODES // 4
    grams[0] = jnp.concatenate([gram[q * quarter : (q + 1) * quarter] for q in range(4)], axis=1)

    def send_gram(j):
        d = sent(nb - 2 - j)
        for dr in range(nr):
            gram_copy(dr, d).start()

    each(0, nb - 1, send_gram)
    each(1, nr, lambda d: gram_copy(d, 0).start())
    each(1, nr * nb, lambda k: gram_copy(k // nb, k % nb).wait_recv())
    packed = jnp.sum(grams[...], axis=0)
    gram = jnp.concatenate([packed[:, q * MODES : (q + 1) * MODES] for q in range(4)], axis=0)

    sub_id = lax.broadcasted_iota(jnp.int32, (MODES, 2 * MODES), 0)
    lane_id = lax.broadcasted_iota(jnp.int32, (MODES, 2 * MODES), 1)
    eye = (sub_id == lane_id).astype(jnp.float32)
    work = jnp.concatenate([eye[:, :MODES], gram], axis=1)
    for k in range(0, MODES, 2):
        c = MODES + k
        first, second = work[k : k + 1], work[k + 1 : k + 2]
        left, right = work[:, c : c + 1], work[:, c + 1 : c + 2]
        scaled = first * (1.0 / work[k : k + 1, c : c + 1])
        cross = scaled[:, c + 1 : c + 2]
        second = second - scaled * work[k + 1 : k + 2, c : c + 1]
        right = right - left * cross
        second = second * (1.0 / second[:, c + 1 : c + 2])
        work = work - jnp.where(sub_id > k, left, 0.0) * scaled - jnp.where(sub_id > k + 1, right, 0.0) * second
    pivots = jnp.sum(jnp.where(lane_id == sub_id + MODES, work, 0.0), axis=1, keepdims=True)
    neurons = float(height * nr * nb)
    inverse = work[:, :MODES] * (math.sqrt(neurons) / jnp.sqrt(pivots))
    out[...] = jnp.dot(
        inverse, image, precision=lax.Precision.HIGHEST, preferred_element_type=jnp.float32
    )

    def sent_cols(d):
        sub_copy(d).wait_send()
        col_copy(d).wait_send()

    def sent_rows(d):
        row_copy(d).wait_send()
        part_copy(d).wait_send()

    each(1, nb, sent_cols)
    each(1, nr, sent_rows)
    each(1, nr * nb, lambda k: gram_copy(k // nb, k % nb).wait_send())


def local(nr, nb, counts, subspace):
    height = counts.shape[0]
    vmem = pl.BlockSpec(memory_space=pltpu.VMEM)
    hbm = pl.BlockSpec(memory_space=pl.ANY)
    dma = pltpu.SemaphoreType.DMA
    modes_t = pl.pallas_call(
        functools.partial(kernel, nr, nb),
        out_shape=jax.ShapeDtypeStruct((MODES, height), jnp.float32),
        in_specs=[hbm, hbm, hbm],
        out_specs=vmem,
        scratch_shapes=[
            pltpu.VMEM((SEGS, height, EPOCH_STEPS), jnp.int32),
            pltpu.VMEM((SEGS * EPOCH_STEPS, 3 * WIDTH), jnp.bfloat16),
            pltpu.VMEM((nr, height, WIDTH), jnp.bfloat16),
            pltpu.VMEM((nr, height, WIDTH), jnp.bfloat16),
            pltpu.VMEM((nr, 8, height), jnp.float32),
            pltpu.VMEM((nb, height, WIDTH), jnp.bfloat16),
            pltpu.VMEM((nb, MODES, height), jnp.bfloat16),
            pltpu.VMEM((nr, MODES, height), jnp.float32),
            pltpu.VMEM((nr, MODES, height), jnp.float32),
            pltpu.VMEM((nr * nb, MODES // 4, 4 * MODES), jnp.float32),
            dma((SEGS,)), dma, dma,
            dma((nr,)), dma((nr,)),
            dma((nb,)), dma((nb,)), dma((nb,)), dma((nb,)),
            dma((nr,)), dma((nr,)),
            dma((nr * nb,)), dma((nr * nb,)),
        ],
        compiler_params=pltpu.CompilerParams(
            collective_id=0, has_side_effects=True, vmem_limit_bytes=58368 * 1024
        ),
        name="subspace_step",
    )(counts, subspace.T, jnp.asarray(split_table()))
    return modes_t.T


def solution(mesh):
    nr, nb = mesh.shape["row"], mesh.shape["blk"]
    return jax.shard_map(
        functools.partial(local, nr, nb),
        mesh=mesh,
        in_specs=(P(("freq", "row", "blk"), None, None), P(("freq", "row", "blk"), None)),
        out_specs=P(("freq", "row", "blk"), None),
        check_vma=False,
    )
```
